32 devices in a mesh: ctx: 16 (over z, x, core), head: 2 (over y).
Axes of the slice: x: 2, y: 2, z: 4, core: 2. Of those that a mesh axis runs over, the one named last changes fastest.
Arguments:
- queries: bfloat16 [8192, 4096], P('ctx', 'head'), may hold values from -17 to 17
- key_rows: bfloat16 [8192, 4096], P('ctx', 'head'), may hold values from -17 to 17
- values: bfloat16 [8192, 4096], P('ctx', 'head'), may hold values from -6 to 6
- out_weight: bfloat16 [4096, 4096], P('head', 'ctx'), may hold values from -0.125 to 0.125
- grad_mixed: bfloat16 [8192, 4096], P('ctx'), may hold values from -6 to 6
- link_mask: int32 [64, 5], P('ctx'), may hold values 0 or 1
Outputs:
- mixed_out: bfloat16 [8192, 4096], P('ctx', 'head')
- grad_query: bfloat16 [8192, 4096], P('ctx', 'head')
- grad_key: bfloat16 [8192, 4096], P('ctx', 'head')
- grad_value: bfloat16 [8192, 4096], P('ctx', 'head')
- grad_out_weight: float32 [4096, 4096], P('head', 'ctx')
The draws below stay inside these ranges and needn't reach their ends.
All inputs are finite; a program needn't handle non-finite values. No bound on the sum of `link_mask` on one device may be relied on, other than what follows from the above.
Results may differ from the reference program's by a relative error of at most 0.02.
Values may be sent and summed in bfloat16 or wider, within the bound.
A program may use at most 384 MiB of HBM per device.

```python
import math
import jax
import jax.numpy as jnp
from jax import lax

D = 4096
HEADS = 32
HEAD_DIM = 128
BLK = 128
LEVELS = 5
TOK_DEV = 512
TOKENS = 8192
BLOCKS = 64
N_CTX = 16
N_HEAD = 2


def draw_queries(key, part):
    key = jax.random.fold_in(key, 11)
    drawn = jnp.clip(jax.random.normal(key, (TOKENS, HEADS * HEAD_DIM), jnp.float32), -4.0, 4.0)
    return drawn.astype(jnp.bfloat16)


def draw_key_rows(key, part):
    key = jax.random.fold_in(key, 12)
    drawn = jnp.clip(jax.random.normal(key, (TOKENS, HEADS * HEAD_DIM), jnp.float32), -4.0, 4.0)
    return drawn.astype(jnp.bfloat16)


def set_ends(result, own_key, smallest, top_value):
    index_at = [jax.random.randint(jax.random.fold_in(own_key, axis), (), 0, length) for axis, length in enumerate(result.shape)]
    main_axis = result.shape.index(max(result.shape))
    beside = index_at[:main_axis] + [(index_at[main_axis] + 1) % result.shape[main_axis]] + index_at[main_axis + 1:]
    return result.at[tuple(index_at)].set(smallest).at[tuple(beside)].set(top_value)


def with_spikes(entries, stream_key, source, target, shards_of, factor):
    def block_of(dim):
        return (jnp.arange(entries.shape[dim]) // (entries.shape[dim] // shards_of)).reshape((-1,) + (1,) * (entries.ndim - 1 - dim))

    one_side = jax.random.permutation(stream_key, shards_of)[block_of(target)]
    far = (block_of(target) + shards_of // 2) % shards_of
    return jnp.where((block_of(source) == one_side) | (block_of(source) == far), factor * entries, entries)


def steps_of(stream_key, shape, pieces, low, largest):
    def one(position, parts):
        heights = jax.random.uniform(jax.random.fold_in(jax.random.fold_in(stream_key, 6), position), (parts,), jnp.float32, low / len(pieces), largest / len(pieces))
        return jnp.repeat(jnp.exp(heights), shape[position] // parts).reshape((-1,) + (1,) * (len(shape) - position - 1))

    factor_of = one(*pieces[0])
    for cut in pieces[1:]:
        factor_of = factor_of * one(*cut)
    return factor_of


def noise(rng, dims, scale, bound, cuts=(), kind=jnp.bfloat16):
    result = jax.random.normal(rng, dims, jnp.float32) * scale
    if len(cuts) > 0:
        result = steps_of(rng, dims, cuts, -0.22, 0.18) * result
    return jnp.clip(result, min=-bound, max=bound).astype(kind)


def heavy_noise(key, extent, deviation, limit, split, heavy, held_as=jnp.bfloat16):
    values = deviation * jax.random.normal(key, extent, jnp.float32)
    if split:
        values = values * steps_of(key, extent, split, -0.22, 0.18)
    return jnp.clip(with_spikes(values, jax.random.fold_in(key, 3), *heavy), -limit, limit).astype(held_as)


def setup_inputs(seed: int = 0) -> dict:
    key_list = jax.random.split(jax.random.key(seed), 7)
    return {
        "queries": draw_queries(jax.random.fold_in(key_list[6], 71), 0),
        "key_rows": draw_key_rows(jax.random.fold_in(key_list[6], 71), 0),
        "values": noise(key_list[2], (TOKENS, HEADS * HEAD_DIM), 1.0, 6.0, ((0, 16), (1, 2))),
        "out_weight": heavy_noise(key_list[3], (HEADS * HEAD_DIM, D), (HEADS * HEAD_DIM) ** -0.5, 0.125, ((0, 2), (1, 16)), (0, 1, 16, 2.0)),
        "grad_mixed": heavy_noise(key_list[4], (TOKENS, D), 1.0, 6.0, ((0, 16),), (0, 1, 16, 2.0)),
        "link_mask": set_ends((jax.random.randint(key_list[5], (BLOCKS, LEVELS), 0, 4) < 3).astype(jnp.int32), jax.random.fold_in(key_list[5], 1), 0, 1),
    }


def as_heads(array):
    return array.reshape(TOKENS, HEADS, HEAD_DIM).transpose(1, 0, 2)

def from_heads(array):
    return array.transpose(1, 0, 2).reshape(TOKENS, HEADS * HEAD_DIM)

def reference(queries, key_rows, values, out_weight, grad_mixed, link_mask):
    score_scale = 1.0 / math.sqrt(HEAD_DIM)
    grad_attn = lax.dot_general(grad_mixed, out_weight, (((1,), (1,)), ((), ())), preferred_element_type=jnp.float32).astype(jnp.bfloat16)
    blk_total = TOKENS // BLK
    span_array = 2 ** jnp.arange(LEVELS, dtype=jnp.int32)
    block_ids = jnp.arange(blk_total, dtype=jnp.int32)
    sources = block_ids[:, None] - span_array[None, :]
    live_link = (sources >= 0) & (link_mask == 1)
    sources = jnp.maximum(sources, 0).astype(jnp.int32)
    positions = jnp.arange(BLK)
    causal = positions[:, None] >= positions[None, :]
    self_ok = jnp.broadcast_to(causal[None, :, None, :], (blk_total, BLK, 1, BLK))
    level_ok = jnp.broadcast_to(live_link[:, None, :, None], (blk_total, BLK, LEVELS, BLK))
    allowed = jnp.concatenate([self_ok, level_ok], 2)

    def one_head(inputs):
        head_query, head_key, head_value, head_grad = inputs

        def blocked(array):
            return array.reshape(blk_total, BLK, HEAD_DIM)
        query_blk = blocked(head_query).astype(jnp.float32)
        key_blk = blocked(head_key)
        value_blk = blocked(head_value)
        key_all = jnp.concatenate([key_blk[:, None], key_blk[sources]], 1).astype(jnp.float32)
        value_all = jnp.concatenate([value_blk[:, None], value_blk[sources]], 1).astype(jnp.float32)
        scores = jnp.einsum('nqe,nlke->nqlk', query_blk, key_all) * score_scale
        scores = jnp.where(allowed, scores, -jnp.inf)
        top_score = lax.optimization_barrier(jnp.max(scores, axis=(2, 3), keepdims=True))
        weights = jnp.exp(scores - top_score)
        prob_full = weights / lax.optimization_barrier(jnp.sum(weights, axis=(2, 3), keepdims=True))
        prob_low = prob_full.astype(jnp.bfloat16).astype(jnp.float32)
        attn_blk = jnp.einsum('nqlk,nlke->nqe', prob_low, value_all).astype(jnp.bfloat16)
        grad_blk = blocked(head_grad).astype(jnp.float32)
        row_delta = lax.optimization_barrier(jnp.sum(grad_blk * attn_blk.astype(jnp.float32), axis=2))[:, :, None, None]
        grad_probs = jnp.einsum('nqe,nlke->nqlk', grad_blk, value_all)
        grad_scores = (prob_full * (grad_probs - row_delta) * score_scale).astype(jnp.bfloat16).astype(jnp.float32)
        grad_q = jnp.einsum('nqlk,nlke->nqe', grad_scores, key_all).astype(jnp.bfloat16)
        key_terms = jnp.einsum('nqlk,nqe->nlke', grad_scores, query_blk)
        value_terms = jnp.einsum('nqlk,nqe->nlke', prob_low, grad_blk)

        def gather_back(term_set):
            spread = jnp.zeros((blk_total, BLK, HEAD_DIM), jnp.float32).at[sources.reshape(-1)].add(term_set[:, 1:].reshape(-1, BLK, HEAD_DIM))
            return (term_set[:, 0] + spread).astype(jnp.bfloat16).reshape(TOKENS, HEAD_DIM)
        return (attn_blk.reshape(TOKENS, HEAD_DIM), grad_q.reshape(TOKENS, HEAD_DIM), gather_back(key_terms), gather_back(value_terms))
    results = lax.map(one_head, (as_heads(queries), as_heads(key_rows), as_heads(values), as_heads(grad_attn)))
    attended, grad_query, grad_key, grad_value = [from_heads(item) for item in results]
    group_width = HEADS * HEAD_DIM // N_HEAD
    mixed_sum = jnp.zeros((TOKENS, D), jnp.float32)
    for group_index in range(N_HEAD):
        lo_col = group_index * group_width
        part_sum = jnp.dot(attended[:, lo_col:lo_col + group_width], out_weight[lo_col:lo_col + group_width], preferred_element_type=jnp.float32)
        mixed_sum = mixed_sum + lax.optimization_barrier(part_sum.astype(jnp.bfloat16)).astype(jnp.float32)
    mixed_out = mixed_sum.astype(jnp.bfloat16)
    attn_shards = attended.reshape(N_CTX, TOK_DEV, HEADS * HEAD_DIM)
    grad_shards = grad_mixed.reshape(N_CTX, TOK_DEV, D)

    def add_shard(carry, shard_pair):
        attn_part, grad_part = shard_pair
        term_sum = lax.dot_general(attn_part, grad_part, (((0,), (0,)), ((), ())), preferred_element_type=jnp.float32)
        return (carry + lax.optimization_barrier(term_sum.astype(jnp.bfloat16)).astype(jnp.float32), None)
    grad_out_weight, unused_tail = lax.scan(add_shard, jnp.zeros((HEADS * HEAD_DIM, D), jnp.float32), (attn_shards, grad_shards))
    return (mixed_out, grad_query, grad_key, grad_value, grad_out_weight)
```

```python
import functools
import math

import jax
import jax.numpy as jnp
from jax import lax
from jax.experimental import pallas as pl
from jax.experimental.pallas import tpu as pltpu
from jax.sharding import PartitionSpec as P

HEAD_DIM = 128
BLK = 128
LEVELS = 5
PAIR = 2
DEAD = -1e30


def passed_along(block, axis, distance):
    devices = range(lax.axis_size(axis))
    route = [(i - distance, i) for i in devices if i - distance in devices]
    return lax.ppermute(block, axis, route)


def reach(block, span, count):
    if span >= count:
        return span // count, block
    if 0 <= block + span < count:
        return 0, block + span
    return 1, (block + span) % count


def reach_back(block, span, count):
    if span >= count:
        return span // count, block
    if block - span >= 0:
        return 0, block - span
    return 1, block - span + count


def rows_of(block):
    return slice(block * BLK, (block + 1) * BLK)


def dot_nt(a, b):
    return lax.dot_general(a, b, (((1,), (1,)), ((), ())), preferred_element_type=jnp.float32)


def dot_nn(a, b):
    return lax.dot_general(a, b, (((1,), (0,)), ((), ())), preferred_element_type=jnp.float32)


def as_row(column):
    return jnp.broadcast_to(column, (BLK, BLK)).T[:1]


def query_side(offsets, scale, live_ref, q_ref, g_ref, *refs):
    sources = [0] + offsets
    keys = {d: refs[2 * n] for n, d in enumerate(sources)}
    vals = {d: refs[2 * n + 1] for n, d in enumerate(sources)}
    att_ref, dq_ref, stat_ref = refs[2 * len(sources):]
    count = q_ref.shape[0] // BLK
    causal = lax.broadcasted_iota(jnp.int32, (BLK, BLK), 0) >= lax.broadcasted_iota(
        jnp.int32, (BLK, BLK), 1
    )
    for h in range(PAIR):
        cols = slice(h * HEAD_DIM, (h + 1) * HEAD_DIM)
        for b in range(count):
            rows = rows_of(b)
            q = q_ref[rows, cols]
            g = g_ref[rows, cols]
            where = [(0, b)] + [reach_back(b, 2**l, count) for l in range(LEVELS)]
            kc = jnp.concatenate([keys[d][rows_of(c), cols] for d, c in where], 0)
            vc = jnp.concatenate([vals[d][rows_of(c), cols] for d, c in where], 0)
            s = dot_nt(q, kc) * scale
            parts = [jnp.where(causal, s[:, :BLK], DEAD)]
            for l in range(LEVELS):
                part = s[:, (l + 1) * BLK : (l + 2) * BLK]
                parts.append(jnp.where(live_ref[b, l] > 0, part, DEAD))
            s = jnp.concatenate(parts, 1)
            top = jnp.max(s, axis=1, keepdims=True)
            w = jnp.exp(s - top)
            total = jnp.sum(w, axis=1, keepdims=True)
            prob = w * (1.0 / total)
            att = dot_nn(prob.astype(jnp.bfloat16), vc).astype(jnp.bfloat16)
            att_ref[rows, cols] = att
            delta = jnp.sum(
                g.astype(jnp.float32) * att.astype(jnp.float32), axis=1, keepdims=True
            )
            ds = (prob * ((dot_nt(g, vc) - delta) * scale)).astype(jnp.bfloat16)
            dq_ref[rows, cols] = dot_nn(ds, kc).astype(jnp.bfloat16)
            stat_ref[0, h : h + 1, rows] = as_row(top + jnp.log(total))
            stat_ref[0, PAIR + h : PAIR + h + 1, rows] = as_row(delta)


def key_side(offsets, scale, link_ref, k_ref, v_ref, *refs):
    sources = [0] + offsets
    quer = {d: refs[3 * n] for n, d in enumerate(sources)}
    grad = {d: refs[3 * n + 1] for n, d in enumerate(sources)}
    stat = {d: refs[3 * n + 2] for n, d in enumerate(sources)}
    at = {d: n for n, d in enumerate(sources)}
    dk_ref, dv_ref = refs[3 * len(sources):]
    count = k_ref.shape[0] // BLK
    causal = lax.broadcasted_iota(jnp.int32, (BLK, BLK), 0) <= lax.broadcasted_iota(
        jnp.int32, (BLK, BLK), 1
    )
    for h in range(PAIR):
        cols = slice(h * HEAD_DIM, (h + 1) * HEAD_DIM)
        for b in range(count):
            rows = rows_of(b)
            k = k_ref[rows, cols]
            v = v_ref[rows, cols]
            where = [(0, b)] + [reach(b, 2**l, count) for l in range(LEVELS)]
            qc = jnp.concatenate([quer[d][rows_of(c), cols] for d, c in where], 0)
            gc = jnp.concatenate([grad[d][rows_of(c), cols] for d, c in where], 0)
            lse = jnp.concatenate([stat[d][0, h : h + 1, rows_of(c)] for d, c in where], 1)
            delta = jnp.concatenate(
                [stat[d][0, PAIR + h : PAIR + h + 1, rows_of(c)] for d, c in where], 1
            )
            s = dot_nt(k, qc) * scale - lse
            parts = [jnp.where(causal, s[:, :BLK], DEAD)]
            for l in range(LEVELS):
                d, c = where[l + 1]
                part = s[:, (l + 1) * BLK : (l + 2) * BLK]
                parts.append(jnp.where(link_ref[at[d] * count + c, l] == 1, part, DEAD))
            prob = jnp.exp(jnp.concatenate(parts, 1))
            dv_ref[rows, cols] = dot_nn(prob.astype(jnp.bfloat16), gc).astype(jnp.bfloat16)
            ds = (prob * ((dot_nt(v, gc) - delta) * scale)).astype(jnp.bfloat16)
            dk_ref[rows, cols] = dot_nn(ds, qc).astype(jnp.bfloat16)


def on_device(queries, key_rows, values, out_weight, grad_mixed, link_mask):
    row_count, col_count = queries.shape
    blk_count = row_count // BLK
    head_count = col_count // HEAD_DIM
    steps = head_count // PAIR
    score_scale = 1.0 / math.sqrt(HEAD_DIM)
    span_list = [2**depth_index for depth_index in range(LEVELS)]
    offsets = sorted(
        set([1] + [span_size // blk_count for span_size in span_list if span_size >= blk_count])
    )
    block_ids = lax.axis_index("ctx") * blk_count + jnp.arange(blk_count, dtype=jnp.int32)
    span_array = jnp.array(span_list, jnp.int32)
    live = ((block_ids[:, None] - span_array[None, :] >= 0) & (link_mask == 1)).astype(jnp.int32)

    weight_full = lax.all_gather(out_weight, "ctx", axis=1, tiled=True)
    kv = [key_rows, values]
    for distance in offsets:
        kv += list(passed_along((key_rows, values), "ctx", distance))
    later_queries = [passed_along(queries, "ctx", -distance) for distance in offsets]
    links = jnp.concatenate(
        [link_mask] + [passed_along(link_mask, "ctx", -distance) for distance in offsets], 0
    )

    grad_attn = lax.dot_general(
        grad_mixed, weight_full, (((1,), (1,)), ((), ())), preferred_element_type=jnp.float32
    ).astype(jnp.bfloat16)
    later_grads = [passed_along(grad_attn, "ctx", -distance) for distance in offsets]

    wide = pl.BlockSpec((row_count, PAIR * HEAD_DIM), lambda i: (0, i))
    narrow = pl.BlockSpec((1, 2 * PAIR, row_count), lambda i: (i, 0, 0))
    scalars = pl.BlockSpec(memory_space=pltpu.SMEM)
    like_rows = jax.ShapeDtypeStruct((row_count, col_count), jnp.bfloat16)
    like_stat = jax.ShapeDtypeStruct((steps, 2 * PAIR, row_count), jnp.float32)
    tiles = blk_count * head_count * (LEVELS + 1)
    cost = pl.CostEstimate(
        flops=4 * 2 * tiles * BLK * BLK * HEAD_DIM * 4,
        bytes_accessed=12 * row_count * col_count * 2,
        transcendentals=tiles * BLK * BLK,
    )
    params = pltpu.CompilerParams(vmem_limit_bytes=48 * 1024 * 1024)
    attended, grad_query, stats = pl.pallas_call(
        functools.partial(query_side, offsets, score_scale),
        grid=(steps,),
        in_specs=[scalars] + [wide] * (2 + len(kv)),
        out_specs=[wide, wide, narrow],
        out_shape=[like_rows, like_rows, like_stat],
        compiler_params=params,
        cost_estimate=cost,
        name="query_side",
    )(live, queries, grad_attn, *kv)
    later_stats = [passed_along(stats, "ctx", -distance) for distance in offsets]

    weight_part = lax.dot_general(
        attended, grad_mixed, (((0,), (0,)), ((), ())), preferred_element_type=jnp.float32
    )
    grad_out_weight = lax.psum_scatter(
        weight_part.astype(jnp.bfloat16), "ctx", scatter_dimension=1, tiled=True
    ).astype(jnp.float32)
    partial_value = jnp.dot(attended, weight_full, preferred_element_type=jnp.float32)
    mixed_out = lax.psum_scatter(
        partial_value.astype(jnp.bfloat16), "head", scatter_dimension=1, tiled=True
    )

    triples = [queries, grad_attn, stats]
    for n in range(len(offsets)):
        triples += [later_queries[n], later_grads[n], later_stats[n]]
    grad_key, grad_value = pl.pallas_call(
        functools.partial(key_side, offsets, score_scale),
        grid=(steps,),
        in_specs=[scalars, wide, wide] + [wide, wide, narrow] * (1 + len(offsets)),
        out_specs=[wide, wide],
        out_shape=[like_rows, like_rows],
        compiler_params=params,
        cost_estimate=cost,
        name="key_side",
    )(links, key_rows, values, *triples)
    return (mixed_out, grad_query, grad_key, grad_value, grad_out_weight)


def solution(mesh):
    placed = (
        P("ctx", "head"),
        P("ctx", "head"),
        P("ctx", "head"),
        P("head", "ctx"),
        P("ctx", None),
        P("ctx", None),
    )
    return jax.shard_map(
        on_device,
        mesh=mesh,
        in_specs=placed,
        out_specs=(
            P("ctx", "head"),
            P("ctx", "head"),
            P("ctx", "head"),
            P("ctx", "head"),
            P("head", "ctx"),
        ),
        check_vma=False,
    )
```

```python
import functools
import math

import jax
import jax.numpy as jnp
from jax import lax
from jax.experimental import pallas as pl
from jax.experimental.pallas import tpu as pltpu
from jax.sharding import PartitionSpec as P

HEAD_DIM = 128
BLK = 128
LEVELS = 5
PIECES = 4
DEAD = -1e30


def passed_along(block, axis, distance):
    devices = range(lax.axis_size(axis))
    route = [(i - distance, i) for i in devices if i - distance in devices]
    return lax.ppermute(block, axis, route)


def rows_of(block):
    return slice(block * BLK, (block + 1) * BLK)


def dot_nt(a, b):
    return lax.dot_general(a, b, (((1,), (1,)), ((), ())), preferred_element_type=jnp.float32)


def dot_nn(a, b):
    return lax.dot_general(a, b, (((1,), (0,)), ((), ())), preferred_element_type=jnp.float32)


def dot_tn(a, b):
    return lax.dot_general(a, b, (((0,), (0,)), ((), ())), preferred_element_type=jnp.float32)


def one_head(scale, at_ref, live_ref, q_ref, g_ref, kv_ref, old_ref, att_ref, dq_ref, dkv_ref, dold_ref, dk_acc, dv_acc):
    at = at_ref[0]
    pieces, length, _ = q_ref.shape
    count = length // BLK
    blocks = pieces * count
    causal = lax.broadcasted_iota(jnp.int32, (BLK, BLK), 0) >= lax.broadcasted_iota(
        jnp.int32, (BLK, BLK), 1
    )

    def load(member, block):
        ref = kv_ref if block >= 0 else old_ref
        block = block % blocks
        return ref[member, (block // count) ^ at, rows_of(block % count), :]

    dk_acc[...] = jnp.zeros_like(dk_acc)
    dv_acc[...] = jnp.zeros_like(dv_acc)
    for t in range(blocks):
        here, rows = (t // count) ^ at, rows_of(t % count)
        q = q_ref[here, rows, :]
        g = g_ref[here, rows, :]
        where = [t] + [t - 2**l for l in range(LEVELS)]
        kc = jnp.concatenate([load(0, c) for c in where], 0)
        vc = jnp.concatenate([load(1, c) for c in where], 0)
        s = dot_nt(q, kc) * scale
        parts = [jnp.where(causal, s[:, :BLK], DEAD)]
        for l in range(LEVELS):
            part = s[:, (l + 1) * BLK : (l + 2) * BLK]
            parts.append(jnp.where(live_ref[t, l] > 0, part, DEAD))
        s = jnp.concatenate(parts, 1)
        top = jnp.max(s, axis=1, keepdims=True)
        w = jnp.exp(s - top)
        prob = w * (1.0 / jnp.sum(w, axis=1, keepdims=True))
        low = prob.astype(jnp.bfloat16)
        att = dot_nn(low, vc).astype(jnp.bfloat16)
        att_ref[here, rows, :] = att
        delta = jnp.sum(g.astype(jnp.float32) * att.astype(jnp.float32), axis=1, keepdims=True)
        ds = (prob * ((dot_nt(g, vc) - delta) * scale)).astype(jnp.bfloat16)
        dq_ref[here, rows, :] = dot_nn(ds, kc).astype(jnp.bfloat16)
        dk = dot_tn(ds, q)
        dv = dot_tn(low, g)
        for n, c in enumerate(where):
            dk_acc[rows_of(c + blocks), :] += dk[rows_of(n), :]
            dv_acc[rows_of(c + blocks), :] += dv[rows_of(n), :]
    for member, acc in enumerate((dk_acc, dv_acc)):
        for p in range(pieces):
            old = slice(p * length, (p + 1) * length)
            own = slice((pieces + p) * length, (pieces + p + 1) * length)
            dold_ref[member, p ^ at, :, :] = acc[old, :].astype(jnp.bfloat16)
            dkv_ref[member, p ^ at, :, :] = acc[own, :].astype(jnp.bfloat16)


def exchanged(block, bit):
    return lax.ppermute(block, "ctx", [(i, i ^ bit) for i in range(lax.axis_size("ctx"))])


def by_distance(grad_mixed):
    rows, width = grad_mixed.shape
    count = lax.axis_size("ctx")
    planes = count // 4
    chunk = width // count
    me = lax.axis_index("ctx")
    plane, side, core = me // 4, (me // 2) % 2, me % 2

    def picked(which):
        owners = [
            ((plane + step) % planes) * 4 + other * 2 + which
            for other in (1 - side, side)
            for step in range(1, planes + 1)
        ]
        return jnp.concatenate(
            [lax.dynamic_slice_in_dim(grad_mixed, owner * chunk, chunk, 1) for owner in owners], 1
        )

    return picked(1 - core), picked(core)


def weight_gradient(attended, columns):
    count = lax.axis_size("ctx")
    planes = count // 4
    chunk = columns[0].shape[1] // (2 * planes)

    def product(picked):
        return lax.dot_general(
            attended, picked, (((0,), (0,)), ((), ())), preferred_element_type=jnp.float32
        ).astype(jnp.bfloat16)

    half = planes * chunk
    arrived = exchanged(product(columns[0]), 1)
    mine = product(columns[1])
    away = (
        mine[:, :half].astype(jnp.float32) + arrived[:, :half].astype(jnp.float32)
    ).astype(jnp.bfloat16)
    came = exchanged(away, 2)
    kept = (
        mine[:, half:].astype(jnp.float32)
        + arrived[:, half:].astype(jnp.float32)
        + came.astype(jnp.float32)
    )
    total = kept[:, (planes - 1) * chunk :]
    sent = kept[:, : (planes - 1) * chunk].astype(jnp.bfloat16)
    for step in range(1, planes):
        part = lax.ppermute(
            sent[:, (step - 1) * chunk : step * chunk],
            "ctx",
            [(i, (i + 4 * step) % count) for i in range(count)],
        )
        total = total + part.astype(jnp.float32)
    return total


def summed_over_heads(attended, weight_full):
    count = lax.axis_size("head")
    me = lax.axis_index("head")
    width = weight_full.shape[1] // count

    def product(which):
        columns = lax.dynamic_slice_in_dim(weight_full, which * width, width, 1)
        return jnp.dot(attended, columns, preferred_element_type=jnp.float32).astype(jnp.bfloat16)

    parts = []
    for step in range(1, count):
        away = product((me + step) % count)
        parts.append(
            lax.ppermute(away, "head", [(i, (i + step) % count) for i in range(count)])
        )
    total = product(me).astype(jnp.float32)
    for part in parts:
        total = total + part.astype(jnp.float32)
    return total.astype(jnp.bfloat16)


def placed_piece(at_ref, from_ref, to_ref):
    to_ref[...] = from_ref[0]


def on_device(queries, key_rows, values, out_weight, grad_mixed, link_mask):
    row_count, col_count = queries.shape
    blk_count = row_count // BLK
    wide = col_count // PIECES
    score_scale = 1.0 / math.sqrt(HEAD_DIM)
    me = lax.axis_index("ctx")
    at = me % PIECES
    others = at ^ jnp.arange(PIECES, dtype=jnp.int32)

    def columns_for(array, piece):
        return lax.dynamic_slice_in_dim(array, (at ^ piece) * wide, wide, 1)

    def to_heads(arrays):
        got = []
        for piece in range(PIECES):
            part = jnp.stack([columns_for(array, piece) for array in arrays], 0)
            got.append(exchanged(part, piece) if piece else part)
        return jnp.stack(got, 1)

    def to_steps(array):
        got = [exchanged(array[piece], piece) if piece else array[piece] for piece in range(PIECES)]
        return pl.pallas_call(
            placed_piece,
            grid_spec=pltpu.PrefetchScalarGridSpec(
                num_scalar_prefetch=1,
                grid=(PIECES,),
                in_specs=[
                    pl.BlockSpec((1, row_count, wide), lambda i, at_ref: (i ^ at_ref[0], 0, 0))
                ],
                out_specs=pl.BlockSpec((row_count, wide), lambda i, at_ref: (0, i)),
            ),
            out_shape=jax.ShapeDtypeStruct((row_count, col_count), jnp.bfloat16),
            name="placed_piece",
        )(at.astype(jnp.int32).reshape(1), jnp.stack(got, 0))

    kv = to_heads([key_rows, values])
    old = passed_along(kv, "ctx", PIECES)
    (query_pieces,) = to_heads([queries])
    links = jnp.stack([exchanged(link_mask, p) if p else link_mask for p in range(PIECES)], 0)
    links = jnp.take(links, others, axis=0).reshape(PIECES * blk_count, LEVELS)
    first = (me // PIECES) * PIECES * blk_count
    block_ids = first + jnp.arange(PIECES * blk_count, dtype=jnp.int32)
    span_array = jnp.array([2**l for l in range(LEVELS)], jnp.int32)
    live = ((block_ids[:, None] - span_array[None, :] >= 0) & (links == 1)).astype(jnp.int32)

    weight_full = lax.all_gather(out_weight, "ctx", axis=1, tiled=True)
    columns = by_distance(grad_mixed)
    weight_full, old, query_pieces, columns, live = lax.optimization_barrier(
        (weight_full, old, query_pieces, columns, live)
    )
    grad_attn = lax.dot_general(
        grad_mixed, weight_full, (((1,), (1,)), ((), ())), preferred_element_type=jnp.float32
    ).astype(jnp.bfloat16)
    (grad_pieces,) = to_heads([grad_attn])

    single = pl.BlockSpec((PIECES, row_count, HEAD_DIM), lambda i: (0, 0, i))
    double = pl.BlockSpec((2, PIECES, row_count, HEAD_DIM), lambda i: (0, 0, 0, i))
    scalars = pl.BlockSpec(memory_space=pltpu.SMEM)
    like_single = jax.ShapeDtypeStruct(query_pieces.shape, jnp.bfloat16)
    like_double = jax.ShapeDtypeStruct(kv.shape, jnp.bfloat16)
    heads = wide // HEAD_DIM
    tiles = PIECES * blk_count * heads * (LEVELS + 1)
    attended, grad_query, grad_kv, grad_old = pl.pallas_call(
        functools.partial(one_head, score_scale),
        grid=(heads,),
        in_specs=[scalars, scalars, single, single, double, double],
        out_specs=[single, single, double, double],
        out_shape=[like_single, like_single, like_double, like_double],
        scratch_shapes=[pltpu.VMEM((2 * PIECES * row_count, HEAD_DIM), jnp.float32)] * 2,
        compiler_params=pltpu.CompilerParams(vmem_limit_bytes=48 * 1024 * 1024),
        cost_estimate=pl.CostEstimate(
            flops=6 * 2 * tiles * BLK * BLK * HEAD_DIM * 4,
            bytes_accessed=12 * row_count * col_count * 2,
            transcendentals=tiles * BLK * BLK,
        ),
        name="one_head",
    )(at.astype(jnp.int32).reshape(1), live, query_pieces, grad_pieces, kv, old)

    attended, grad_query, grad_kv, grad_old = lax.optimization_barrier(
        (to_steps(attended), grad_query, grad_kv, grad_old)
    )
    owed = passed_along(grad_old, "ctx", -PIECES)
    grad_out_weight = weight_gradient(attended, columns)
    mixed_out = summed_over_heads(attended, weight_full)
    grad_query = to_steps(grad_query)
    total = (grad_kv.astype(jnp.float32) + owed.astype(jnp.float32)).astype(jnp.bfloat16)
    return (mixed_out, grad_query, to_steps(total[0]), to_steps(total[1]), grad_out_weight)


def solution(mesh):
    placed = (
        P("ctx", "head"),
        P("ctx", "head"),
        P("ctx", "head"),
        P("head", "ctx"),
        P("ctx", None),
        P("ctx", None),
    )
    return jax.shard_map(
        on_device,
        mesh=mesh,
        in_specs=placed,
        out_specs=(
            P("ctx", "head"),
            P("ctx", "head"),
            P("ctx", "head"),
            P("ctx", "head"),
            P("head", "ctx"),
        ),
        check_vma=False,
    )
```
